32 devices in a mesh: row: 4 (over y, core), col: 8 (over z, x).
Axes of the slice: x: 2, y: 2, z: 4, core: 2. Of those that a mesh axis runs over, the one named last changes fastest.
Arguments:
- sigma_top: float32 [8192, 8192], P('row', 'col')
- panel: float32 [4, 8192, 512], P(None, ('row', 'col')), may hold values from -0.0007324219 to 0.0007324219
- parent_panel: float32 [3, 512, 512], replicated, may hold values from -0.1875 to 0.1875
- diag_inverse: float32 [4, 512, 512], replicated, as said below
- block_depth: int32 [64], replicated, may hold values from 0 to 4, as said below
Outputs:
- sigma_cols: float32 [4, 8192, 512], P(None, ('row', 'col'))
- sigma_link: float32 [3, 512, 512], P(None, 'row')
- sigma_diag: float32 [4, 512, 512], P(None, 'row')
The draws below stay inside these ranges and needn't reach their ends.
Inputs may be any that keep to these rules, and one draw needn't show every extreme that they name: Ancestor rows are nested: supernode k holds block b among its ancestor rows exactly when block_depth[b] > k. Each diag_inverse[k] is lower triangular. sigma_top is symmetric: sigma_top[i, j] = sigma_top[j, i] exactly.
All inputs are finite; a program needn't handle non-finite values.
Results may differ from the reference program's by a relative error of at most 0.0001.
Values sent between devices are 32-bit elements; how exact they have to be, the bound alone decides.
A program may use at most 128 MiB of HBM per device.

```python
import math
import jax
import jax.numpy as jnp
from jax import lax

ANC = 8192
W = 512
STEPS = 4
BLOCK = 128
NBLK = 64


def draw_sigma_top(key, part):
    key = jax.random.fold_in(key, 11)
    noise_key, level_key = jax.random.split(key)
    noise = jax.random.normal(noise_key, (ANC, ANC), jnp.float32)
    level = jnp.exp(jax.random.uniform(level_key, (ANC,), jnp.float32, math.log(0.5), math.log(2.0)))
    spread_vals = (noise + noise.T) * (0.22 * math.sqrt(ANC) / math.sqrt(2.0))
    return spread_vals + jnp.diag(level * ANC)


def draw_diag_inverse(key, part):
    key = jax.random.fold_in(key, 23)
    noise_key, lead_key = jax.random.split(key)
    below_mask = (jnp.arange(W)[:, None] > jnp.arange(W)[None, :]).astype(jnp.float32)
    noise = jax.random.normal(noise_key, (STEPS, W, W), jnp.float32)
    leading = jnp.exp(jax.random.uniform(lead_key, (STEPS, W), jnp.float32, math.log(0.7), math.log(1.4)))
    return noise * below_mask * (0.4 / math.sqrt(W)) + jnp.eye(W, dtype=jnp.float32) * leading[:, None, :]


def draw_block_depth(key, part):
    key = jax.random.fold_in(key, 37)
    order = jax.random.permutation(key, NBLK)
    return (order % (STEPS + 1)).astype(jnp.int32)


def levels(rng, shape, shards, least, high):
    def one(dim, blocks):
        heights = jax.random.uniform(jax.random.fold_in(jax.random.fold_in(rng, 6), dim), (blocks,), jnp.float32, least / len(shards), high / len(shards))
        return jnp.repeat(jnp.exp(heights), shape[dim] // blocks).reshape((-1,) + (1,) * (len(shape) - dim - 1))

    factor_of = one(*shards[0])
    for cut in shards[1:]:
        factor_of = factor_of * one(*cut)
    return factor_of


def centred(stream_key, dims, scale, bound, cuts=(), kind=jnp.bfloat16):
    result = scale * jax.random.normal(stream_key, dims, jnp.float32)
    if cuts:
        result = result * levels(stream_key, dims, cuts, -0.22, 0.18)
    return jnp.clip(result, -bound, bound).astype(kind)


def setup_inputs(seed: int = 0) -> dict:
    key_of = jax.random.split(jax.random.key(seed), 6)
    sigma_top = draw_sigma_top(jax.random.fold_in(key_of[5], 71), 0)
    panel = centred(key_of[1], (STEPS, ANC, W), (ANC * ANC) ** -0.5, 0.0007324219, ((1, 32),), jnp.float32)
    parent_panel = centred(key_of[2], (STEPS - 1, W, W), (2 * W) ** -0.5, 0.1875, (), jnp.float32)
    diag_inverse = draw_diag_inverse(jax.random.fold_in(key_of[5], 71), 0)
    block_depth = draw_block_depth(jax.random.fold_in(key_of[5], 71), 0)
    return dict(sigma_top=sigma_top, panel=panel, parent_panel=parent_panel, diag_inverse=diag_inverse, block_depth=block_depth)


def reference(sigma_top, panel, parent_panel, diag_inverse, block_depth):
    highest = lax.Precision.HIGHEST
    row_blocks = jnp.arange(ANC, dtype=jnp.int32) // BLOCK
    depth_rows = block_depth[row_blocks]
    column_list = []
    link_list = []
    diagonals = []
    for section in range(STEPS):
        row_mask = jnp.where(depth_rows > section, 1.0, 0.0).astype(jnp.float32)[:, None]
        masked_panel = row_mask * panel[section]
        product = jnp.dot(sigma_top, masked_panel, precision=highest)
        inverse = diag_inverse[section]
        diag_block = jnp.dot(inverse.T, inverse, precision=highest)
        if section > 0:
            parent = parent_panel[section - 1]
            earlier = column_list[-1]
            product = product + jnp.dot(earlier, parent, precision=highest)
            crossed = jnp.dot(earlier.T, masked_panel, precision=highest)
            link_block = -(crossed + jnp.dot(diagonals[-1], parent, precision=highest))
            link_list.append(link_block)
        new_cols = -row_mask * product
        diag_block = diag_block - jnp.dot(masked_panel.T, new_cols, precision=highest)
        if section > 0:
            diag_block = diag_block - jnp.dot(parent.T, link_list[-1], precision=highest)
        column_list.append(new_cols)
        diagonals.append(diag_block)
    return jnp.stack(column_list), jnp.stack(link_list), jnp.stack(diagonals)
```

```python
import jax
import jax.numpy as jnp
from jax import lax
from jax.sharding import PartitionSpec as P

STEPS = 4
BLOCK = 128
HIGH = lax.Precision.HIGH


def dot(a, b):
    return jnp.dot(a, b, precision=HIGH, preferred_element_type=jnp.float32)


def dot_t(a, b):
    return lax.dot_general(
        a, b, (((0,), (0,)), ((), ())), precision=HIGH, preferred_element_type=jnp.float32
    )


def split(value):
    upper = lax.reduce_precision(value, 8, 7)
    return upper.astype(jnp.bfloat16), (value - upper).astype(jnp.bfloat16)


def row_depth(block_depth, first_row, row_total):
    blocks = (first_row + jnp.arange(row_total, dtype=jnp.int32)) // BLOCK
    block_ids = jnp.arange(block_depth.shape[0], dtype=jnp.int32)
    matched = (blocks[:, None] == block_ids[None, :]).astype(jnp.int32)
    return jnp.sum(matched * block_depth[None, :], axis=1)


def pick(value, which):
    return lax.dynamic_index_in_dim(value, which, 1, keepdims=False)


def shards(sigma_top, panel, parent_panel, diag_inverse, block_depth):
    row_count = lax.axis_size("row")
    col_count = lax.axis_size("col")
    row_index = lax.axis_index("row")
    col_index = lax.axis_index("col")
    share = panel.shape[1]
    width = panel.shape[2]
    depth = sigma_top.shape[1]
    out_rows = width // row_count
    own_depth = row_depth(block_depth, (row_index * col_count + col_index) * share, share)
    own_masks = [
        jnp.where(own_depth > k, 1.0, 0.0).astype(jnp.float32)[:, None] for k in range(STEPS)
    ]
    masked = [own_masks[k] * panel[k] for k in range(STEPS)]

    swap = [
        (g, (g % row_count) * col_count + g // row_count) for g in range(row_count * col_count)
    ]
    right = []
    for k in range(STEPS):
        part = lax.ppermute(masked[k], ("row", "col"), swap)
        whole = lax.all_gather(part, "row", axis=0, tiled=True)
        upper, lower = split(whole)
        right.append(jnp.concatenate([upper, upper, lower], axis=0))

    pairs = sigma_top.reshape(col_count // 2, 2, share, depth)
    bit = col_index % 2
    left = []
    for which in (1 - bit, bit):
        upper, lower = split(pick(pairs, which).reshape(col_count // 2 * share, depth))
        left.append(jnp.concatenate([upper, lower, upper], axis=1))

    def exchange(value, stage):
        return lax.ppermute(value, "col", [(c, c ^ (1 << stage)) for c in range(col_count)])

    products = []
    for k in range(STEPS):
        gone = jnp.dot(left[0], right[k], preferred_element_type=jnp.float32)
        gone = exchange(gone, 0)
        total = jnp.dot(left[1], right[k], preferred_element_type=jnp.float32) + gone
        stage = 1
        while (1 << stage) < col_count:
            bit = (col_index >> stage) % 2
            pieces = total.reshape(total.shape[0] // (2 * share), 2, share, width)
            gone = exchange(pick(pieces, 1 - bit), stage)
            total = (pick(pieces, bit) + gone).reshape(-1, width)
            stage += 1
        products.append(total)

    columns = []
    links = []
    diagonals = []
    token = None
    for k in range(STEPS):
        summed = products[k]
        if k > 0:
            summed = summed + dot(columns[-1], parent_panel[k - 1])
        columns.append(-own_masks[k] * summed)
        parts = [dot_t(masked[k], columns[k])]
        if k > 0:
            parts.append(dot_t(columns[k - 1], masked[k]))
        parts = jnp.stack(parts)
        if token is not None:
            parts, token = lax.optimization_barrier((parts, token))
        token = lax.psum(parts, ("row", "col"))
        diagonal = dot_t(diag_inverse[k], diag_inverse[k]) - token[0]
        if k > 0:
            parent = parent_panel[k - 1]
            links.append(-(token[1] + dot(diagonals[-1], parent)))
            diagonal = diagonal - dot_t(parent, links[-1])
        diagonals.append(diagonal)
    link_stack = lax.dynamic_slice_in_dim(jnp.stack(links), row_index * out_rows, out_rows, 1)
    diag_stack = lax.dynamic_slice_in_dim(jnp.stack(diagonals), row_index * out_rows, out_rows, 1)
    return (jnp.stack(columns), link_stack, diag_stack)


def solution(mesh):
    return jax.shard_map(
        shards,
        mesh=mesh,
        in_specs=(P("row", "col"), P(None, ("row", "col"), None), P(), P(), P()),
        out_specs=(P(None, ("row", "col"), None), P(None, "row", None), P(None, "row", None)),
        check_vma=False,
    )
```

```python
import jax
import jax.numpy as jnp
from jax import lax
from jax.sharding import PartitionSpec as P

STEPS = 4
BLOCK = 128
HIGH = lax.Precision.HIGH


def dot(a, b):
    return jnp.dot(a, b, precision=HIGH, preferred_element_type=jnp.float32)


def dot_t(a, b):
    return lax.dot_general(
        a, b, (((0,), (0,)), ((), ())), precision=HIGH, preferred_element_type=jnp.float32
    )


def split(value):
    upper = lax.reduce_precision(value, 8, 7)
    return upper.astype(jnp.bfloat16), (value - upper).astype(jnp.bfloat16)


def row_depth(block_depth, first_row, row_total):
    blocks = (first_row + jnp.arange(row_total, dtype=jnp.int32)) // BLOCK
    block_ids = jnp.arange(block_depth.shape[0], dtype=jnp.int32)
    matched = (blocks[:, None] == block_ids[None, :]).astype(jnp.int32)
    return jnp.sum(matched * block_depth[None, :], axis=1)


def after(value, earlier):
    if earlier is None:
        return value
    return lax.optimization_barrier((value, earlier))[0]


def pick(value, which):
    return lax.dynamic_index_in_dim(value, which, 1, keepdims=False)


def shards(sigma_top, panel, parent_panel, diag_inverse, block_depth):
    row_count = lax.axis_size("row")
    col_count = lax.axis_size("col")
    row_index = lax.axis_index("row")
    col_index = lax.axis_index("col")
    share = panel.shape[1]
    width = panel.shape[2]
    depth = sigma_top.shape[1]
    out_rows = width // row_count
    own_depth = row_depth(block_depth, (row_index * col_count + col_index) * share, share)
    own_masks = [
        jnp.where(own_depth > k, 1.0, 0.0).astype(jnp.float32)[:, None] for k in range(STEPS)
    ]
    masked = [own_masks[k] * panel[k] for k in range(STEPS)]

    swap = [
        (g, (g % row_count) * col_count + g // row_count) for g in range(row_count * col_count)
    ]
    right = []
    part = None
    for k in range(STEPS):
        part = lax.ppermute(after(masked[k], part), ("row", "col"), swap)
        whole = lax.all_gather(part, "row", axis=0, tiled=True)
        upper, lower = split(whole)
        right.append(jnp.concatenate([upper, upper, lower], axis=0))

    pairs = sigma_top.reshape(col_count // 2, 2, share, depth)
    bit = col_index % 2
    left = []
    for which in (1 - bit, bit):
        upper, lower = split(pick(pairs, which).reshape(col_count // 2 * share, depth))
        left.append(jnp.concatenate([upper, lower, upper], axis=1))

    def exchange(value, axis, stage):
        count = lax.axis_size(axis)
        return lax.ppermute(value, axis, [(i, i ^ (1 << stage)) for i in range(count)])

    def reduce_slab(parts):
        for stage in range(row_count.bit_length() - 1):
            halves = parts.reshape(parts.shape[0], -1, 2, out_rows, width)
            bit = (row_index >> stage) % 2
            gone = lax.dynamic_index_in_dim(halves, 1 - bit, 2, keepdims=False)
            kept = lax.dynamic_index_in_dim(halves, bit, 2, keepdims=False)
            parts = kept + exchange(gone, "row", stage)
        parts = parts.reshape(-1, out_rows, width)
        for stage in range(col_count.bit_length() - 1):
            parts = parts + exchange(parts, "col", stage)
        return parts

    columns = []
    diag_sums = []
    cross_sums = []
    nearer = []
    for k in range(STEPS):
        gone = jnp.dot(left[0], right[k], preferred_element_type=jnp.float32)
        gone = exchange(after(gone, nearer[k - 2] if k > 1 else None), "col", 0)
        total = jnp.dot(left[1], right[k], preferred_element_type=jnp.float32) + gone
        for stage in range(1, col_count.bit_length() - 1):
            bit = (col_index >> stage) % 2
            pieces = total.reshape(total.shape[0] // (2 * share), 2, share, width)
            gone = exchange(pick(pieces, 1 - bit), "col", stage)
            total = (pick(pieces, bit) + gone).reshape(-1, width)
            if stage == 1:
                nearer.append(gone)
        if k > 0:
            total = total + dot(columns[-1], parent_panel[k - 1])
        columns.append(-own_masks[k] * total)
        parts = [dot_t(masked[k], columns[k])]
        if k + 1 < STEPS:
            parts.append(dot_t(columns[k], masked[k + 1]))
        slab = reduce_slab(jnp.stack(parts))
        if k + 1 < STEPS:
            sums = lax.all_gather(slab, "row", axis=1, tiled=True)
            diag_sums.append(sums[0])
            cross_sums.append(sums[1])

    def own_slab(value):
        return lax.dynamic_slice_in_dim(value, row_index * out_rows, out_rows, 0)

    def own_columns(value):
        return lax.dynamic_slice_in_dim(value, row_index * out_rows, out_rows, 1)

    links = []
    diagonals = []
    for k in range(STEPS - 1):
        diagonal = dot_t(diag_inverse[k], diag_inverse[k]) - diag_sums[k]
        if k > 0:
            diagonal = diagonal - dot_t(parent_panel[k - 1], links[-1])
        diagonals.append(diagonal)
        links.append(-(cross_sums[k] + dot(diagonal, parent_panel[k])))
    last = dot_t(own_columns(diag_inverse[-1]), diag_inverse[-1])
    last = last - dot_t(own_columns(parent_panel[-1]), links[-1]) - slab[0]
    return (
        jnp.stack(columns),
        jnp.stack([own_slab(value) for value in links]),
        jnp.stack([own_slab(value) for value in diagonals] + [last]),
    )


def solution(mesh):
    return jax.shard_map(
        shards,
        mesh=mesh,
        in_specs=(P("row", "col"), P(None, ("row", "col"), None), P(), P(), P()),
        out_specs=(P(None, ("row", "col"), None), P(None, "row", None), P(None, "row", None)),
        check_vma=False,
    )
```

```python
import jax
import jax.numpy as jnp
from jax import lax
from jax.sharding import PartitionSpec as P

STEPS = 4
BLOCK = 128
HIGH = lax.Precision.HIGH


def dot(a, b):
    return jnp.dot(a, b, precision=HIGH, preferred_element_type=jnp.float32)


def dot_t(a, b):
    return lax.dot_general(
        a, b, (((0,), (0,)), ((), ())), precision=HIGH, preferred_element_type=jnp.float32
    )


def split(value):
    upper = lax.reduce_precision(value, 8, 7)
    return upper.astype(jnp.bfloat16), (value - upper).astype(jnp.bfloat16)


def row_depth(block_depth, first_row, row_total):
    blocks = (first_row + jnp.arange(row_total, dtype=jnp.int32)) // BLOCK
    block_ids = jnp.arange(block_depth.shape[0], dtype=jnp.int32)
    matched = (blocks[:, None] == block_ids[None, :]).astype(jnp.int32)
    return jnp.sum(matched * block_depth[None, :], axis=1)


def after(value, earlier):
    if earlier is None:
        return value
    return lax.optimization_barrier((value, earlier))[0]


def pick(value, which):
    return lax.dynamic_index_in_dim(value, which, 1, keepdims=False)


def shards(sigma_top, panel, parent_panel, diag_inverse, block_depth):
    row_count = lax.axis_size("row")
    col_count = lax.axis_size("col")
    row_index = lax.axis_index("row")
    col_index = lax.axis_index("col")
    share = panel.shape[1]
    width = panel.shape[2]
    depth = sigma_top.shape[1]
    out_rows = width // row_count
    own_depth = row_depth(block_depth, (row_index * col_count + col_index) * share, share)
    own_masks = [
        jnp.where(own_depth > k, 1.0, 0.0).astype(jnp.float32)[:, None] for k in range(STEPS)
    ]
    masked = [own_masks[k] * panel[k] for k in range(STEPS)]

    swap = [
        (g, (g % row_count) * col_count + g // row_count) for g in range(row_count * col_count)
    ]
    right = []
    part = None
    for k in range(STEPS):
        part = lax.ppermute(after(masked[k], part), ("row", "col"), swap)
        whole = lax.all_gather(part, "row", axis=0, tiled=True)
        upper, lower = split(whole)
        right.append(jnp.concatenate([upper, upper, lower], axis=0))

    pairs = sigma_top.reshape(col_count // 2, 2, share, depth)
    bit = col_index % 2
    left = []
    for which in (1 - bit, bit):
        upper, lower = split(pick(pairs, which).reshape(col_count // 2 * share, depth))
        left.append(jnp.concatenate([upper, lower, upper], axis=1))

    def exchange(value, axis, stage):
        count = lax.axis_size(axis)
        return lax.ppermute(value, axis, [(i, i ^ (1 << stage)) for i in range(count)])

    def reduce_slab(parts):
        for stage in range(row_count.bit_length() - 1):
            halves = parts.reshape(parts.shape[0], -1, 2, out_rows, width)
            bit = (row_index >> stage) % 2
            gone = lax.dynamic_index_in_dim(halves, 1 - bit, 2, keepdims=False)
            kept = lax.dynamic_index_in_dim(halves, bit, 2, keepdims=False)
            parts = kept + exchange(gone, "row", stage)
        parts = parts.reshape(-1, out_rows, width)
        for stage in range(col_count.bit_length() - 1):
            parts = parts + exchange(parts, "col", stage)
        return parts

    columns = []
    nearer = []
    parts = []
    early = STEPS - 3
    for k in range(STEPS):
        gone = jnp.dot(left[0], right[k], preferred_element_type=jnp.float32)
        gone = exchange(after(gone, nearer[k - 2] if k > 1 else None), "col", 0)
        total = jnp.dot(left[1], right[k], preferred_element_type=jnp.float32) + gone
        for stage in range(1, col_count.bit_length() - 1):
            bit = (col_index >> stage) % 2
            pieces = total.reshape(total.shape[0] // (2 * share), 2, share, width)
            gone = exchange(pick(pieces, 1 - bit), "col", stage)
            total = (pick(pieces, bit) + gone).reshape(-1, width)
            if stage == 1:
                nearer.append(gone)
        if k > 0:
            total = total + dot(columns[-1], parent_panel[k - 1])
        columns.append(-own_masks[k] * total)
        parts.append(dot_t(masked[k], columns[k]))
        if k + 1 < STEPS:
            parts.append(dot_t(columns[k], masked[k + 1]))
        if k == early:
            nearer[k] = parts = jnp.stack(parts)
            sums = lax.psum(parts, ("row", "col"))
            parts = []
        elif k > early:
            slab = reduce_slab(jnp.stack(parts))
            parts = []
            if k + 1 < STEPS:
                sums = jnp.concatenate([sums, lax.all_gather(slab, "row", axis=1, tiled=True)])
    diag_sums = sums[0::2]
    cross_sums = sums[1::2]

    def own_slab(value):
        return lax.dynamic_slice_in_dim(value, row_index * out_rows, out_rows, 0)

    def own_columns(value):
        return lax.dynamic_slice_in_dim(value, row_index * out_rows, out_rows, 1)

    links = []
    diagonals = []
    for k in range(STEPS - 1):
        diagonal = dot_t(diag_inverse[k], diag_inverse[k]) - diag_sums[k]
        if k > 0:
            diagonal = diagonal - dot_t(parent_panel[k - 1], links[-1])
        diagonals.append(diagonal)
        links.append(-(cross_sums[k] + dot(diagonal, parent_panel[k])))
    last = dot_t(own_columns(diag_inverse[-1]), diag_inverse[-1])
    last = last - dot_t(own_columns(parent_panel[-1]), links[-1]) - slab[0]
    return (
        jnp.stack(columns),
        jnp.stack([own_slab(value) for value in links]),
        jnp.stack([own_slab(value) for value in diagonals] + [last]),
    )


def solution(mesh):
    return jax.shard_map(
        shards,
        mesh=mesh,
        in_specs=(P("row", "col"), P(None, ("row", "col"), None), P(), P(), P()),
        out_specs=(P(None, ("row", "col"), None), P(None, "row", None), P(None, "row", None)),
        check_vma=False,
    )
```

```python
import jax
import jax.numpy as jnp
from jax import lax
from jax.sharding import PartitionSpec as P

STEPS = 4
BLOCK = 128
HIGH = lax.Precision.HIGH


def dot(a, b):
    return jnp.dot(a, b, precision=HIGH, preferred_element_type=jnp.float32)


def dot_t(a, b):
    return lax.dot_general(
        a, b, (((0,), (0,)), ((), ())), precision=HIGH, preferred_element_type=jnp.float32
    )


def split(value):
    upper = lax.reduce_precision(value, 8, 7)
    return upper.astype(jnp.bfloat16), (value - upper).astype(jnp.bfloat16)


def row_depth(block_depth, first_row, row_total):
    blocks = (first_row + jnp.arange(row_total, dtype=jnp.int32)) // BLOCK
    block_ids = jnp.arange(block_depth.shape[0], dtype=jnp.int32)
    matched = (blocks[:, None] == block_ids[None, :]).astype(jnp.int32)
    return jnp.sum(matched * block_depth[None, :], axis=1)


def after(value, earlier):
    if earlier is None:
        return value
    return lax.optimization_barrier((value, earlier))[0]


def pick(value, which):
    return lax.dynamic_index_in_dim(value, which, 1, keepdims=False)


def shards(sigma_top, panel, parent_panel, diag_inverse, block_depth):
    row_count = lax.axis_size("row")
    col_count = lax.axis_size("col")
    row_index = lax.axis_index("row")
    col_index = lax.axis_index("col")
    share = panel.shape[1]
    width = panel.shape[2]
    depth = sigma_top.shape[1]
    out_rows = width // row_count
    own_depth = row_depth(block_depth, (row_index * col_count + col_index) * share, share)
    own_masks = [
        jnp.where(own_depth > k, 1.0, 0.0).astype(jnp.float32)[:, None] for k in range(STEPS)
    ]
    masked = [own_masks[k] * panel[k] for k in range(STEPS)]

    swap = [
        (g, (g % row_count) * col_count + g // row_count) for g in range(row_count * col_count)
    ]
    right = []
    part = None
    for k in range(STEPS):
        part = lax.ppermute(after(masked[k], part), ("row", "col"), swap)
        whole = lax.all_gather(part, "row", axis=0, tiled=True)
        upper, lower = split(whole)
        right.append(jnp.concatenate([upper, upper, lower], axis=0))

    pairs = sigma_top.reshape(col_count // 2, 2, share, depth)
    bit = col_index % 2
    left = []
    for which in (1 - bit, bit):
        upper, lower = split(pick(pairs, which).reshape(col_count // 2 * share, depth))
        left.append(jnp.concatenate([upper, lower, upper], axis=1))

    def exchange(value, axis, stage):
        count = lax.axis_size(axis)
        return lax.ppermute(value, axis, [(i, i ^ (1 << stage)) for i in range(count)])

    def reduce_slab(parts):
        for stage in range(row_count.bit_length() - 1):
            halves = parts.reshape(parts.shape[0], -1, 2, out_rows, width)
            bit = (row_index >> stage) % 2
            gone = lax.dynamic_index_in_dim(halves, 1 - bit, 2, keepdims=False)
            kept = lax.dynamic_index_in_dim(halves, bit, 2, keepdims=False)
            parts = kept + exchange(gone, "row", stage)
        parts = parts.reshape(-1, out_rows, width)
        for stage in range(col_count.bit_length() - 1):
            parts = parts + exchange(parts, "col", stage)
        return parts

    columns = []
    nearer = []
    parts = []
    early = STEPS - 3
    for k in range(STEPS):
        gone = jnp.dot(left[0], right[k], preferred_element_type=jnp.float32)
        gone = exchange(after(gone, nearer[k - 2] if k > 1 else None), "col", 0)
        nearer.append(gone)
        total = jnp.dot(left[1], right[k], preferred_element_type=jnp.float32) + gone
        for stage in range(1, col_count.bit_length() - 1):
            bit = (col_index >> stage) % 2
            pieces = total.reshape(total.shape[0] // (2 * share), 2, share, width)
            gone = exchange(pick(pieces, 1 - bit), "col", stage)
            total = (pick(pieces, bit) + gone).reshape(-1, width)
        if k > 0:
            total = total + dot(columns[-1], parent_panel[k - 1])
        columns.append(-own_masks[k] * total)
        parts.append(dot_t(masked[k], columns[k]))
        if k + 1 < STEPS:
            parts.append(dot_t(columns[k], masked[k + 1]))
        if k == early:
            sums = lax.psum_scatter(jnp.stack(parts), "row", scatter_dimension=1, tiled=True)
            sums = lax.all_gather(lax.psum(sums, "col"), "row", axis=1, tiled=True)
            parts = []
        elif k > early:
            slab = reduce_slab(jnp.stack(parts))
            parts = []
            if k + 1 < STEPS:
                sums = jnp.concatenate([sums, lax.all_gather(slab, "row", axis=1, tiled=True)])
    diag_sums = sums[0::2]
    cross_sums = sums[1::2]

    def own_slab(value):
        return lax.dynamic_slice_in_dim(value, row_index * out_rows, out_rows, 0)

    def own_columns(value):
        return lax.dynamic_slice_in_dim(value, row_index * out_rows, out_rows, 1)

    links = []
    diagonals = []
    for k in range(STEPS - 1):
        diagonal = dot_t(diag_inverse[k], diag_inverse[k]) - diag_sums[k]
        if k > 0:
            diagonal = diagonal - dot_t(parent_panel[k - 1], links[-1])
        diagonals.append(diagonal)
        links.append(-(cross_sums[k] + dot(diagonal, parent_panel[k])))
    last = dot_t(own_columns(diag_inverse[-1]), diag_inverse[-1])
    last = last - dot_t(own_columns(parent_panel[-1]), links[-1]) - slab[0]
    return (
        jnp.stack(columns),
        jnp.stack([own_slab(value) for value in links]),
        jnp.stack([own_slab(value) for value in diagonals] + [last]),
    )


def solution(mesh):
    return jax.shard_map(
        shards,
        mesh=mesh,
        in_specs=(P("row", "col"), P(None, ("row", "col"), None), P(), P(), P()),
        out_specs=(P(None, ("row", "col"), None), P(None, "row", None), P(None, "row", None)),
        check_vma=False,
    )
```

```python
import jax
import jax.numpy as jnp
from jax import lax
from jax.sharding import PartitionSpec as P

STEPS = 4
BLOCK = 128
HIGH = lax.Precision.HIGH


def dot(a, b):
    return jnp.dot(a, b, precision=HIGH, preferred_element_type=jnp.float32)


def dot_t(a, b):
    return lax.dot_general(
        a, b, (((0,), (0,)), ((), ())), precision=HIGH, preferred_element_type=jnp.float32
    )


def split(value):
    upper = lax.reduce_precision(value, 8, 7)
    return upper.astype(jnp.bfloat16), (value - upper).astype(jnp.bfloat16)


def row_depth(block_depth, first_row, row_total):
    blocks = (first_row + jnp.arange(row_total, dtype=jnp.int32)) // BLOCK
    block_ids = jnp.arange(block_depth.shape[0], dtype=jnp.int32)
    matched = (blocks[:, None] == block_ids[None, :]).astype(jnp.int32)
    return jnp.sum(matched * block_depth[None, :], axis=1)


def after(value, earlier):
    if earlier is None:
        return value
    return lax.optimization_barrier((value, earlier))[0]


def pick(value, which):
    return lax.dynamic_index_in_dim(value, which, 1, keepdims=False)


def shards(sigma_top, panel, parent_panel, diag_inverse, block_depth):
    row_count = lax.axis_size("row")
    col_count = lax.axis_size("col")
    row_index = lax.axis_index("row")
    col_index = lax.axis_index("col")
    share = panel.shape[1]
    width = panel.shape[2]
    depth = sigma_top.shape[1]
    out_rows = width // row_count
    own_depth = row_depth(block_depth, (row_index * col_count + col_index) * share, share)
    own_masks = [
        jnp.where(own_depth > k, 1.0, 0.0).astype(jnp.float32)[:, None] for k in range(STEPS)
    ]
    masked = [own_masks[k] * panel[k] for k in range(STEPS)]

    swap = [
        (g, (g % row_count) * col_count + g // row_count) for g in range(row_count * col_count)
    ]
    right = []
    part = None
    for k in range(STEPS):
        part = lax.ppermute(after(masked[k], part), ("row", "col"), swap)
        whole = lax.all_gather(part, "row", axis=0, tiled=True)
        upper, lower = split(whole)
        right.append(jnp.concatenate([upper, upper, lower], axis=0))

    pairs = sigma_top.reshape(col_count // 2, 2, share, depth)
    bit = col_index % 2
    left = []
    for which in (1 - bit, bit):
        upper, lower = split(pick(pairs, which).reshape(col_count // 2 * share, depth))
        left.append(jnp.concatenate([upper, lower, upper], axis=1))

    def exchange(value, axis, stage):
        count = lax.axis_size(axis)
        return lax.ppermute(value, axis, [(i, i ^ (1 << stage)) for i in range(count)])

    def reduce_slab(parts):
        for stage in range(row_count.bit_length() - 1):
            halves = parts.reshape(parts.shape[0], -1, 2, out_rows, width)
            bit = (row_index >> stage) % 2
            gone = lax.dynamic_index_in_dim(halves, 1 - bit, 2, keepdims=False)
            kept = lax.dynamic_index_in_dim(halves, bit, 2, keepdims=False)
            parts = kept + exchange(gone, "row", stage)
        parts = parts.reshape(-1, out_rows, width)
        for stage in range(col_count.bit_length() - 1):
            parts = parts + exchange(parts, "col", stage)
        return parts

    columns = []
    def first_exchange(k, earlier):
        gone = jnp.dot(left[0], right[k], preferred_element_type=jnp.float32)
        return exchange(after(gone, earlier), "col", 0)

    parts = []
    arrived = [first_exchange(0, None), first_exchange(1, None)]
    for k in range(STEPS):
        total = jnp.dot(left[1], right[k], preferred_element_type=jnp.float32) + arrived[k]
        for stage in range(1, col_count.bit_length() - 1):
            bit = (col_index >> stage) % 2
            pieces = total.reshape(total.shape[0] // (2 * share), 2, share, width)
            gone = exchange(pick(pieces, 1 - bit), "col", stage)
            total = (pick(pieces, bit) + gone).reshape(-1, width)
            if stage == 1 and k + 2 < STEPS:
                arrived.append(first_exchange(k + 2, gone))
        if k > 0:
            total = total + dot(columns[-1], parent_panel[k - 1])
        columns.append(-own_masks[k] * total)
        parts.append(dot_t(masked[k], columns[k]))
        if k + 1 < STEPS:
            parts.append(dot_t(columns[k], masked[k + 1]))
        if k == STEPS - 2:
            sums = lax.psum(after(jnp.stack(parts), arrived[-1]), ("row", "col"))
            parts = []
    slab = reduce_slab(jnp.stack(parts))
    diag_sums = sums[0::2]
    cross_sums = sums[1::2]

    def own_slab(value):
        return lax.dynamic_slice_in_dim(value, row_index * out_rows, out_rows, 0)

    def own_columns(value):
        return lax.dynamic_slice_in_dim(value, row_index * out_rows, out_rows, 1)

    offsets = [lax.optimization_barrier(dot_t(value, value)) for value in diag_inverse[:-1]]
    links = []
    diagonals = []
    for k in range(STEPS - 1):
        diagonal = offsets[k] - diag_sums[k]
        if k > 0:
            diagonal = diagonal - dot_t(parent_panel[k - 1], links[-1])
        diagonals.append(diagonal)
        links.append(-(cross_sums[k] + dot(diagonal, parent_panel[k])))
    last = lax.optimization_barrier(
        dot_t(own_columns(diag_inverse[-1]), diag_inverse[-1]) - slab[0]
    )
    last = last - dot_t(own_columns(parent_panel[-1]), links[-1])
    return (
        jnp.stack(columns),
        jnp.stack([own_slab(value) for value in links]),
        jnp.stack([own_slab(value) for value in diagonals] + [last]),
    )


def solution(mesh):
    return jax.shard_map(
        shards,
        mesh=mesh,
        in_specs=(P("row", "col"), P(None, ("row", "col"), None), P(), P(), P()),
        out_specs=(P(None, ("row", "col"), None), P(None, "row", None), P(None, "row", None)),
        check_vma=False,
    )
```
